512 devices in a mesh: section: 16 (over y, core), expert: 32 (over z, x).
Axes of the slice: x: 4, y: 8, z: 8, core: 2. Of those that a mesh axis runs over, the one named last changes fastest.
Arguments:
- pending: bfloat16 [2, 16, 2048, 3584], P(None, 'section', 'expert'), may hold values from -6 to 6
- routes: int32 [2, 16, 2048, 1], P(None, 'section', 'expert'), may hold values from 0 to 3; in each aligned block of 64 rows (0 to 63, 64 to 127, ..., all dimensions but the last counted through in order) at most 16 rows name the same one
- probs: bfloat16 [2, 16, 2048], P(None, 'section', 'expert'), may hold values from 0.049804688 to 0.94921875
- saved_gate: bfloat16 [2, 16, 32, 32, 16, 128], P(None, 'section', 'expert'), may hold values from -6 to 6
- saved_up: bfloat16 [2, 16, 32, 32, 16, 128], P(None, 'section', 'expert'), may hold values from -6 to 6
- w_gate: bfloat16 [16, 3584, 4096], P('section', None, 'expert'), may hold values from -0.09375 to 0.09375
- w_up: bfloat16 [16, 3584, 4096], P('section', None, 'expert'), may hold values from -0.09375 to 0.09375
- w_down: bfloat16 [16, 4096, 3584], P('section', 'expert'), may hold values from -0.09375 to 0.09375
- w_router: float32 [16, 3584, 4], P('section'), may hold values from -0.2 to 0.2
Outputs:
- passed: bfloat16 [2, 16, 2048, 3584], P(None, 'section', 'expert')
The draws below stay inside these ranges and needn't reach their ends.
Inputs may be any that keep to these rules, and one draw needn't show every extreme that they name: `routes`: among the 64 tokens of one device, at one section and direction, each expert is chosen by exactly 16 tokens.
All inputs are finite; a program needn't handle non-finite values.
Results may differ from the reference program's by a relative error of at most 0.0031.
Values may be sent and summed in bfloat16 or wider, within the bound.
No kernel may reach another device: no remote copies, remote signals or barrier semaphores. Data moves between devices by JAX's collectives and lax.ppermute only.
A program may use at most 64 MiB of HBM per device.

```python
import math
import jax
import jax.numpy as jnp
import numpy as np
from jax import lax

D = 3584
HS = 128
EXP_FLIGHT = 4
TOK_DEV = 64
H = 1024
CAP = 16
SECTIONS = 16
TOKENS = 2048
N_EXPERT = 32


def block_levels(stream_key, dims, cuts, low, top_value):
    def one(position, blocks):
        steps = jax.random.uniform(jax.random.fold_in(jax.random.fold_in(stream_key, 6), position), (blocks,), jnp.float32, low / len(cuts), top_value / len(cuts))
        return jnp.repeat(jnp.exp(steps), dims[position] // blocks).reshape((-1,) + (1,) * (len(dims) - position - 1))

    gain = one(*cuts[0])
    for cut in cuts[1:]:
        gain = gain * one(*cut)
    return gain


def routed_block(stream_key, own, number, rows, amount, top, most, lean):
    order = jax.random.permutation(stream_key, amount)
    heavy_load, common = portions_of(amount, rows * top, most, lean, True), portions_of(amount, rows * top, most, lean, False)
    places = jnp.arange(amount)

    def named(lengths, turn):
        used = int((lengths > 0).sum())
        fixed = max(1, used // 4)
        shifted = fixed + (places - fixed + turn * (used - fixed)) % max(1, amount - fixed)
        return jnp.zeros((amount,), jnp.int32).at[order[jnp.where(places < fixed, places, shifted)]].set(jnp.asarray(lengths, jnp.int32))

    lengths = jnp.where(number % 4 == 0, named(heavy_load, number // 4), named(common, number - number // 4 - 1))
    mixed = jax.random.permutation(jax.random.fold_in(own, 3), amount)
    giver, receiver = mixed[0:amount // 2 * 2:2], mixed[1:amount // 2 * 2:2]
    slack = jnp.minimum(lengths[giver] - 1, most - lengths[receiver]) // 2
    slack = jnp.where((giver == order[0]) | (receiver == order[0]) | (lengths[receiver] == 0), 0, jnp.maximum(slack, 0))
    shifted = jax.random.randint(jax.random.fold_in(own, 4), (amount // 2,), 0, 1 << 20) % (slack + 1)
    lengths = lengths.at[giver].add(-shifted).at[receiver].add(shifted)
    members = jnp.searchsorted(jnp.cumsum(lengths), jnp.arange(rows * top), side="right").astype(jnp.int32)
    table = members.reshape(top, rows).T
    table = table[jax.random.permutation(jax.random.fold_in(own, 1), rows)]
    turn = jax.random.randint(jax.random.fold_in(own, 2), (rows, 1), 0, top)
    return jnp.take_along_axis(table, (jnp.arange(top)[None, :] + turn) % top, axis=1)


def portions_of(number_of, total, bound, lean, full):
    portions = [(1 << 20) // math.isqrt(standing ** lean) + 1 for standing in range(1, number_of + 1)]
    largest = bound if full else min(bound, max(-(-total // number_of), total * portions[0] // sum(portions)))
    least = 1 if total - largest >= number_of - 1 else 0
    given, surplus = [largest] + [least] * (number_of - 1), total - largest - least * (number_of - 1)
    while surplus > 0:
        free = [i for i in range(1, number_of) if given[i] < largest] or [i for i in range(1, number_of) if given[i] < bound]
        pool, budget = sum([portions[i] for i in free]), surplus
        for i in free:
            addition = min(bound - given[i], max(1, budget * portions[i] // pool), surplus)
            given[i] = given[i] + addition
            surplus = surplus - addition
    return np.array(given)


def centred(own_key, shape, width, bound, pieces=(), kind=jnp.bfloat16):
    result = jax.random.normal(own_key, shape, jnp.float32) * width
    if len(pieces) > 0:
        result = block_levels(own_key, shape, pieces, -0.22, 0.18) * result
    return jnp.clip(result, min=-bound, max=bound).astype(kind)


def setup_inputs(seed: int = 0) -> dict:
    arg_keys = jax.random.split(jax.random.key(seed), 10)
    pending = centred(arg_keys[0], (2, SECTIONS, TOKENS, D), 1.0, 6.0, ((1, 16), (2, 32)))
    routes_keys = jax.random.split(jax.random.fold_in(arg_keys[1], 1), 2 * SECTIONS * TOKENS // TOK_DEV)
    routes_turns = jax.random.permutation(jax.random.fold_in(arg_keys[1], 3), 2 * SECTIONS * TOKENS // TOK_DEV)
    routes = jax.vmap(lambda own, number: routed_block(jax.random.fold_in(arg_keys[1], 2), own, number, TOK_DEV, EXP_FLIGHT, 1, CAP, 0))(routes_keys, routes_turns).reshape((2, SECTIONS, TOKENS, 1))
    probs = jnp.clip(0.049804688 + 0.89941406 * jax.random.uniform(arg_keys[2], (2, SECTIONS, TOKENS), jnp.float32) ** block_levels(arg_keys[2], (2, SECTIONS, TOKENS), ((1, 16), (2, 32)), -0.2, 0.2), 0.049804688, 0.94921875).astype(jnp.bfloat16)
    saved_gate = centred(arg_keys[3], (2, SECTIONS, N_EXPERT, N_EXPERT, CAP, HS), 1.5, 6.0, ((1, 16), (2, 32)))
    saved_up = centred(arg_keys[4], (2, SECTIONS, N_EXPERT, N_EXPERT, CAP, HS), 1.0, 6.0, ((1, 16), (2, 32)))
    w_gate = centred(arg_keys[5], (SECTIONS, D, EXP_FLIGHT * H), D ** -0.5, 0.09375, ((0, 16), (2, 32)))
    w_up = centred(arg_keys[6], (SECTIONS, D, EXP_FLIGHT * H), D ** -0.5, 0.09375, ((0, 16), (2, 32)))
    w_down = centred(arg_keys[7], (SECTIONS, EXP_FLIGHT * H, D), D ** -0.5, 0.09375, ((0, 16), (1, 32)))
    w_router = centred(arg_keys[8], (SECTIONS, D, EXP_FLIGHT), 0.03, 0.2, ((0, 16),), jnp.float32)
    return {"pending": pending, "routes": routes, "probs": probs, "saved_gate": saved_gate, "saved_up": saved_up, "w_gate": w_gate, "w_up": w_up, "w_down": w_down, "w_router": w_router}


def expert_rows(packed):
    rows, gate_pre, up_pre, prob, wg_e, wu_e, wd_e = packed
    grad_z = jnp.einsum('md,jkd->mjk', rows.astype(jnp.float32), wd_e.astype(jnp.float32))
    sig = jax.nn.sigmoid(gate_pre)
    hidden = gate_pre * sig * up_pre
    dots = jnp.sum(hidden * grad_z, axis=2).astype(jnp.bfloat16)
    dots = lax.optimization_barrier(dots).astype(jnp.float32)
    grad_h = prob[:, None, None] * grad_z
    grad_gate = (grad_h * up_pre * sig * (1.0 + gate_pre * (1.0 - sig))).astype(jnp.bfloat16)
    grad_up = (grad_h * gate_pre * sig).astype(jnp.bfloat16)
    parts = jnp.einsum('mjk,djk->mjd', grad_gate.astype(jnp.float32), wg_e.astype(jnp.float32))
    parts = parts + jnp.einsum('mjk,djk->mjd', grad_up.astype(jnp.float32), wu_e.astype(jnp.float32))
    parts = lax.optimization_barrier(parts.astype(jnp.bfloat16)).astype(jnp.float32)
    return jnp.sum(parts, axis=1), jnp.sum(dots, axis=1)


def layer_back(grad_in, expert_ids, prob, gate_saved, up_saved, wg, wu, wd, wr):
    group = N_EXPERT // EXP_FLIGHT
    per_dev = expert_ids.reshape(N_EXPERT, TOK_DEV)
    onehot = (per_dev[:, :, None] == jnp.arange(EXP_FLIGHT, dtype=jnp.int32)[None, None, :]).astype(jnp.int32)
    slot_index = jnp.sum((jnp.cumsum(onehot, axis=1) - 1) * onehot, axis=2).reshape(TOKENS).astype(jnp.int32)
    source = (jnp.arange(TOKENS, dtype=jnp.int32) // TOK_DEV).astype(jnp.int32)
    gate_r = gate_saved.reshape(EXP_FLIGHT, group, N_EXPERT, CAP, HS)
    up_r = up_saved.reshape(EXP_FLIGHT, group, N_EXPERT, CAP, HS)
    gate_tok = gate_r[expert_ids, :, source, slot_index, :].astype(jnp.float32)
    up_tok = up_r[expert_ids, :, source, slot_index, :].astype(jnp.float32)
    order = jnp.argsort(expert_ids, stable=True).astype(jnp.int32)
    count = TOKENS // EXP_FLIGHT
    prob_f = prob.astype(jnp.float32)
    packed = (grad_in[order].reshape(EXP_FLIGHT, count, D),
              gate_tok[order].reshape(EXP_FLIGHT, count, group, HS),
              up_tok[order].reshape(EXP_FLIGHT, count, group, HS),
              prob_f[order].reshape(EXP_FLIGHT, count),
              jnp.transpose(wg.reshape(D, EXP_FLIGHT, group, HS), (1, 0, 2, 3)),
              jnp.transpose(wu.reshape(D, EXP_FLIGHT, group, HS), (1, 0, 2, 3)),
              wd.reshape(EXP_FLIGHT, group, HS, D))
    back_sorted, dot_sorted = lax.map(expert_rows, packed)
    inverse = jnp.argsort(order).astype(jnp.int32)
    back = back_sorted.reshape(TOKENS, D)[inverse]
    dotsum = dot_sorted.reshape(TOKENS)[inverse]
    scaled = dotsum * prob_f * (1.0 - prob_f)
    router_term = scaled[:, None] * jnp.transpose(wr)[expert_ids]
    return (grad_in.astype(jnp.float32) + back + router_term).astype(jnp.bfloat16)


def reference(pending, routes, probs, saved_gate, saved_up, w_gate, w_up, w_down, w_router):
    results = []
    for direction in range(2):
        section_out = []
        for section in range(SECTIONS):
            if direction == 0:
                anchor = (section + 1) % SECTIONS
            else:
                anchor = (section - 1) % SECTIONS
            section_out.append(layer_back(pending[direction, anchor], routes[direction, section, :, 0],
                                        probs[direction, section], saved_gate[direction, section],
                                        saved_up[direction, section], w_gate[section], w_up[section],
                                        w_down[section], w_router[section]))
        results.append(jnp.stack(section_out))
    return jnp.stack(results)
```

```python
import functools

import jax
import jax.numpy as jnp
from jax import lax
from jax.experimental import pallas as pl
from jax.experimental.pallas import tpu as pltpu
from jax.sharding import PartitionSpec as P

BF = jnp.bfloat16
F32 = jnp.float32
LANE = 128
RING = 4
VMEM_LIMIT = 48 * 1024 * 1024


def shifted(value, axis, steps):
    count = lax.axis_size(axis)
    pairs = [(source, (source + steps) % count) for source in range(count)]
    return lax.ppermute(value, axis, pairs)


def turned(value, steps):
    count = lax.axis_size("expert")
    pairs = [(i, i - i % RING + (i + steps) % RING) for i in range(count)]
    return lax.ppermute(value, "expert", pairs)


def columns(count):
    return [[z * RING + x for z in range(count // RING)] for x in range(RING)]


def rows(count):
    return [[z * RING + x for x in range(RING)] for z in range(count // RING)]


def dot(a, b, contract):
    return lax.dot_general(a, b, ((contract[0], contract[1]), ((), ())), preferred_element_type=F32)


def selection(routes, copies, capacity, experts):
    count = routes.shape[0]
    width = experts * copies * capacity
    code = lax.broadcasted_iota(jnp.int32, (count, width), 1)
    chosen = routes == code // (copies * capacity)
    row = lax.broadcasted_iota(jnp.int32, (count, count), 0)
    col = lax.broadcasted_iota(jnp.int32, (count, count), 1)
    earlier = jnp.where(col < row, 1.0, 0.0).astype(BF)
    before = dot(earlier, jnp.where(chosen, 1.0, 0.0).astype(BF), ((1,), (0,)))
    return jnp.where(chosen & (before.astype(jnp.int32) == code % capacity), 1.0, 0.0)


def pick_kernel(experts, capacity, routes_ref, probs_ref, *rest):
    grads, outs = rest[:2], rest[2:]
    for way in range(2):
        tokens, width = grads[way].shape
        select = selection(routes_ref[way, 0], 1, capacity, experts)
        prob_row = jnp.broadcast_to(probs_ref[way].astype(F32), (tokens, tokens))
        row = lax.broadcasted_iota(jnp.int32, (tokens, tokens), 0)
        col = lax.broadcasted_iota(jnp.int32, (tokens, tokens), 1)
        prob_diag = jnp.where(row == col, prob_row, 0.0).astype(BF)
        select = select.astype(BF)
        prob = jnp.sum(dot(select, prob_diag, ((0,), (0,))), axis=1, keepdims=True)
        prob = jnp.broadcast_to(prob, (tokens, LANE)).astype(BF)
        step = width // RING
        for part in range(RING):
            span = slice(part * step, (part + 1) * step)
            picked = dot(select, grads[way][:, span], ((0,), (0,))).astype(BF)
            for place in range(2 * experts):
                first = place // 2 * capacity
                outs[way][place, :, span] = picked[first : first + capacity]
        for place in range(2 * experts):
            first = place // 2 * capacity
            outs[way][place, :, width:] = prob[first : first + capacity]


def pick(grads, routes, probs, experts, capacity):
    tokens, width = grads[0].shape
    return pl.pallas_call(
        functools.partial(pick_kernel, experts, capacity),
        out_shape=[jax.ShapeDtypeStruct((2 * experts, capacity, width + LANE), BF)] * 2,
        compiler_params=pltpu.CompilerParams(vmem_limit_bytes=VMEM_LIMIT),
        cost_estimate=pl.CostEstimate(flops=10**8, bytes_accessed=4 * 10**6, transcendentals=0),
    )(routes, probs, *grads)


def saved_kernel(gate_ref, up_ref, out_ref):
    planes, ring, capacity, units = gate_ref.shape[1:]
    for x in range(ring):
        for way in range(2):
            out_ref[x, way, 0] = gate_ref[way, :, x].reshape(planes * capacity, units)
            out_ref[x, way, 1] = up_ref[way, :, x].reshape(planes * capacity, units)


def saved_blocks(gate, up):
    _, senders, capacity, units = gate.shape
    planes = senders // RING
    gate = gate.reshape(2, planes, RING, capacity, units)
    up = up.reshape(2, planes, RING, capacity, units)
    return pl.pallas_call(
        saved_kernel,
        out_shape=jax.ShapeDtypeStruct((RING, 2, 2, planes * capacity, units), BF),
        compiler_params=pltpu.CompilerParams(vmem_limit_bytes=VMEM_LIMIT),
        cost_estimate=pl.CostEstimate(flops=0, bytes_accessed=2 * 10**6, transcendentals=0),
    )(gate, up)


def hidden_kernel(
    way, place_ref, tok_ref, saved_ref, own_ref, left_ref, right_ref, low_ref, high_ref, *outs
):
    grads_ref, scaled_ref = outs
    planes, capacity, wide = tok_ref.shape
    width = wide - LANE
    count = planes * capacity
    units = saved_ref.shape[4]
    tok = tok_ref[...].reshape(count, wide)
    prob = tok[:, width:].astype(F32)
    total = jnp.zeros((count, units), F32)
    far = jnp.concatenate([low_ref[...], high_ref[...]], axis=0)
    for step, down in enumerate((own_ref[...], right_ref[...], far, left_ref[...])):
        owner = lax.rem(place_ref[0] + step, RING)
        z = dot(tok[:, :width], down, ((1,), (1,)))
        a = saved_ref[owner, way, 0].astype(F32)
        b = saved_ref[owner, way, 1].astype(F32)
        sig = jax.nn.sigmoid(a)
        act = a * sig
        total = total + act * b * z
        u = prob * z
        grad_gate = u * b * sig * (1.0 + a * (1.0 - sig))
        grads_ref[:, 2 * step * units : (2 * step + 1) * units] = grad_gate.astype(BF)
        grads_ref[:, (2 * step + 1) * units : (2 * step + 2) * units] = (u * act).astype(BF)
    scaled_ref[...] = jnp.sum(total, axis=1, keepdims=True) * (prob * (1.0 - prob))


def hidden_grads(way, place, tok, saved, down):
    planes, capacity, _ = tok.shape
    count, units = planes * capacity, saved.shape[4]
    whole = pl.BlockSpec(memory_space=pltpu.VMEM)
    return pl.pallas_call(
        functools.partial(hidden_kernel, way),
        in_specs=[pl.BlockSpec(memory_space=pltpu.SMEM)] + [whole] * (2 + len(down)),
        out_shape=[
            jax.ShapeDtypeStruct((count, 2 * RING * units), BF),
            jax.ShapeDtypeStruct((count, LANE), F32),
        ],
        compiler_params=pltpu.CompilerParams(vmem_limit_bytes=VMEM_LIMIT),
        cost_estimate=pl.CostEstimate(
            flops=5 * 10**8, bytes_accessed=5 * 10**6, transcendentals=10**5
        ),
    )(place, tok, saved, *down)


def part_kernel(
    first_ref,
    first_scaled_ref,
    second_ref,
    second_scaled_ref,
    router_ref,
    own_ref,
    left_ref,
    right_ref,
    gate_ref,
    up_ref,
    out_ref,
):
    planes, two, width = out_ref.shape
    capacity = two // 2
    count = planes * capacity
    units = own_ref.shape[2]
    grads = jnp.concatenate([first_ref[...], second_ref[...]], axis=0)
    scaled = jnp.concatenate([first_scaled_ref[...], second_scaled_ref[...]], axis=0)[:, :1]
    block = width // 2
    for part in range(2):
        span = slice(part * block, (part + 1) * block)
        weights = (
            own_ref[0, span],
            own_ref[1, span],
            right_ref[0, span],
            right_ref[1, span],
            gate_ref[span],
            up_ref[span],
            left_ref[0, span],
            left_ref[1, span],
        )
        weights = jnp.concatenate(weights, axis=1)
        total = dot(grads, weights, ((1,), (1,))) + scaled * router_ref[:, span]
        total = total.astype(BF)
        for way in range(2):
            piece = total[way * count : (way + 1) * count].reshape(planes, capacity, block)
            out_ref[:, way * capacity : (way + 1) * capacity, span] = piece


def input_parts(grads, router, weights, capacity):
    (first, first_scaled), (second, second_scaled) = grads
    width = router.shape[1]
    whole = pl.BlockSpec(memory_space=pltpu.VMEM)
    return pl.pallas_call(
        part_kernel,
        in_specs=[whole] * (5 + len(weights)),
        out_shape=jax.ShapeDtypeStruct((first.shape[0] // capacity, 2 * capacity, width), BF),
        compiler_params=pltpu.CompilerParams(vmem_limit_bytes=VMEM_LIMIT),
        cost_estimate=pl.CostEstimate(flops=10**9, bytes_accessed=5 * 10**6, transcendentals=0),
    )(first, first_scaled, second, second_scaled, router, *weights)


def finish_kernel(experts, capacity, routes_ref, first_ref, second_ref, back_ref, *rest):
    out_ref = rest[-1]
    planes, _, width = back_ref.shape
    for way, grad_ref in enumerate((first_ref, second_ref)):
        select = selection(routes_ref[way, 0], planes // experts, capacity, experts).astype(BF)
        back = back_ref[:, way * capacity : (way + 1) * capacity].reshape(planes * capacity, width)
        back = dot(select, back, ((1,), (0,)))
        out_ref[way] = (grad_ref[...].astype(F32) + back).astype(BF)


def finish(part, routes, grads, back, experts, capacity, before):
    tokens, width = grads[0].shape
    block = back.shape[2]
    operands = [routes, *grads, back]
    specs = [
        pl.BlockSpec(routes.shape, lambda i: (0, 0, 0, 0)),
        pl.BlockSpec((tokens, block), lambda i: (0, part)),
        pl.BlockSpec((tokens, block), lambda i: (0, part)),
        pl.BlockSpec(back.shape, lambda i: (0, 0, 0)),
    ]
    aliases = {}
    if before is not None:
        operands.append(before)
        specs.append(pl.BlockSpec(memory_space=pl.ANY))
        aliases = {4: 0}
    return pl.pallas_call(
        functools.partial(finish_kernel, experts, capacity),
        grid=(1,),
        in_specs=specs,
        out_specs=pl.BlockSpec((2, tokens, block), lambda i: (0, 0, part)),
        out_shape=jax.ShapeDtypeStruct((2, tokens, width), BF),
        input_output_aliases=aliases,
        compiler_params=pltpu.CompilerParams(vmem_limit_bytes=VMEM_LIMIT),
        cost_estimate=pl.CostEstimate(flops=10**8, bytes_accessed=3 * 10**6, transcendentals=0),
    )(*operands)


def per_device(pending, routes, probs, saved_gate, saved_up, w_gate, w_up, w_down, w_router):
    members = lax.axis_size("expert")
    experts = w_router.shape[2]
    capacity = pending.shape[2] // experts
    me = lax.axis_index("expert")
    place = lax.rem(me, RING).reshape(1).astype(jnp.int32)
    expert = me // (members // experts)
    along_z, along_x = columns(members), rows(members)

    def exchange(value, groups):
        return lax.all_to_all(
            value, "expert", split_axis=0, concat_axis=0, axis_index_groups=groups, tiled=True
        )

    incoming = (shifted(pending[0, 0], "section", -1), shifted(pending[1, 0], "section", 1))
    saved = exchange(saved_blocks(saved_gate[:, 0, 0], saved_up[:, 0, 0]), along_x)

    width = w_gate.shape[1] // 2
    spans = [slice(part * width, (part + 1) * width) for part in range(2)]
    half = w_down.shape[1] // 2
    own = w_down[0]
    left, right = turned(own, 1), turned(own, RING - 1)
    sent = list(pick(incoming, routes, probs, experts, capacity))
    sent[0], saved, left, right = lax.optimization_barrier((sent[0], saved, left, right))
    down = (own, left, right, turned(left[:half], 1), turned(right[half:], RING - 1))

    own = jnp.stack([w_gate[0, spans[0]], w_up[0, spans[0]]])
    left, right = turned(own, 1), turned(own, RING - 1)
    sent[1], left, right = lax.optimization_barrier((sent[1], left, right))
    weights = [(own, left, right, turned(left[0], 1), turned(right[1], RING - 1))]

    own = jnp.stack([w_gate[0, spans[1]], w_up[0, spans[1]]])
    own, down = lax.optimization_barrier((own, down))
    left, right = turned(own, 1), turned(own, RING - 1)
    weights.append((own, left, right, turned(left[0], 1), turned(right[1], RING - 1)))
    router = lax.dynamic_slice(w_router[0], (0, expert), (2 * width, 1)).reshape(1, 2 * width)

    toks = [exchange(sent[way], along_z) for way in range(2)]
    grads = [hidden_grads(way, place, toks[way], saved, down) for way in range(2)]
    out = None
    for part in range(2):
        parts = input_parts(grads, router[:, spans[part]], weights[part], capacity)
        back = exchange(parts, along_z)
        out = finish(part, routes, incoming, back, experts, capacity, out)
    return out[:, None]


def solution(mesh):
    in_specs = (
        P(None, "section", "expert", None),
        P(None, "section", "expert", None),
        P(None, "section", "expert"),
        P(None, "section", "expert", None, None, None),
        P(None, "section", "expert", None, None, None),
        P("section", None, "expert"),
        P("section", None, "expert"),
        P("section", "expert", None),
        P("section", None, None),
    )
    out_specs = P(None, "section", "expert", None)
    return jax.shard_map(
        per_device, mesh=mesh, in_specs=in_specs, out_specs=out_specs, check_vma=False
    )
```

```python
import functools

import jax
import jax.numpy as jnp
from jax import lax
from jax.experimental import pallas as pl
from jax.experimental.pallas import tpu as pltpu
from jax.sharding import PartitionSpec as P

BF = jnp.bfloat16
F32 = jnp.float32
LANE = 128
FLOPS = (10000000000, 1000000000)
RING = 4
VMEM_LIMIT = 48 * 1024 * 1024


def shifted(value, axis, steps):
    count = lax.axis_size(axis)
    pairs = [(source, (source + steps) % count) for source in range(count)]
    return lax.ppermute(value, axis, pairs)


def turned(value, steps):
    count = lax.axis_size("expert")
    pairs = [(i, i - i % RING + (i + steps) % RING) for i in range(count)]
    return lax.ppermute(value, "expert", pairs)


def columns(count):
    return [[z * RING + x for z in range(count // RING)] for x in range(RING)]


def rows(count):
    return [[z * RING + x for x in range(RING)] for z in range(count // RING)]


def dot(a, b, contract):
    return lax.dot_general(a, b, ((contract[0], contract[1]), ((), ())), preferred_element_type=F32)


def selection(routes, copies, capacity, experts):
    count = routes.shape[0]
    width = experts * copies * capacity
    code = lax.broadcasted_iota(jnp.int32, (count, width), 1)
    chosen = routes == code // (copies * capacity)
    row = lax.broadcasted_iota(jnp.int32, (count, count), 0)
    col = lax.broadcasted_iota(jnp.int32, (count, count), 1)
    earlier = jnp.where(col < row, 1.0, 0.0).astype(BF)
    before = dot(earlier, jnp.where(chosen, 1.0, 0.0).astype(BF), ((1,), (0,)))
    return jnp.where(chosen & (before.astype(jnp.int32) == code % capacity), 1.0, 0.0)


def pick_kernel(experts, capacity, routes_ref, probs_ref, *rest):
    grads, outs = rest[:2], rest[2:]
    for way in range(2):
        tokens, width = grads[way].shape
        select = selection(routes_ref[way, 0], 1, capacity, experts)
        prob_row = jnp.broadcast_to(probs_ref[way].astype(F32), (tokens, tokens))
        row = lax.broadcasted_iota(jnp.int32, (tokens, tokens), 0)
        col = lax.broadcasted_iota(jnp.int32, (tokens, tokens), 1)
        prob_diag = jnp.where(row == col, prob_row, 0.0).astype(BF)
        select = select.astype(BF)
        prob = jnp.sum(dot(select, prob_diag, ((0,), (0,))), axis=1, keepdims=True)
        prob = jnp.broadcast_to(prob, (tokens, LANE)).astype(BF)
        step = width // RING
        for part in range(RING):
            span = slice(part * step, (part + 1) * step)
            picked = dot(select, grads[way][:, span], ((0,), (0,))).astype(BF)
            for place in range(2 * experts):
                first = place // 2 * capacity
                outs[way][place, :, span] = picked[first : first + capacity]
        for place in range(2 * experts):
            first = place // 2 * capacity
            outs[way][place, :, width:] = prob[first : first + capacity]


def pick(grads, routes, probs, experts, capacity):
    tokens, width = grads[0].shape
    return pl.pallas_call(
        functools.partial(pick_kernel, experts, capacity),
        out_shape=[jax.ShapeDtypeStruct((2 * experts, capacity, width + LANE), BF)] * 2,
        compiler_params=pltpu.CompilerParams(vmem_limit_bytes=VMEM_LIMIT),
        cost_estimate=pl.CostEstimate(flops=10**8, bytes_accessed=4 * 10**6, transcendentals=0),
    )(routes, probs, *grads)


def saved_kernel(gate_ref, up_ref, out_ref):
    planes, ring, capacity, units = gate_ref.shape[1:]
    for x in range(ring):
        for way in range(2):
            out_ref[x, way, 0] = gate_ref[way, :, x].reshape(planes * capacity, units)
            out_ref[x, way, 1] = up_ref[way, :, x].reshape(planes * capacity, units)


def saved_blocks(gate, up):
    _, senders, capacity, units = gate.shape
    planes = senders // RING
    gate = gate.reshape(2, planes, RING, capacity, units)
    up = up.reshape(2, planes, RING, capacity, units)
    return pl.pallas_call(
        saved_kernel,
        out_shape=jax.ShapeDtypeStruct((RING, 2, 2, planes * capacity, units), BF),
        compiler_params=pltpu.CompilerParams(vmem_limit_bytes=VMEM_LIMIT),
        cost_estimate=pl.CostEstimate(flops=0, bytes_accessed=2 * 10**6, transcendentals=0),
    )(gate, up)


def hidden_kernel(
    way, place_ref, tok_ref, saved_ref, own_ref, left_ref, right_ref, low_ref, high_ref, *outs
):
    grads_ref, scaled_ref = outs
    planes, capacity, wide = tok_ref.shape
    width = wide - LANE
    count = planes * capacity
    units = saved_ref.shape[4]
    tok = tok_ref[...].reshape(count, wide)
    prob = tok[:, width:].astype(F32)
    total = jnp.zeros((count, units), F32)
    far = jnp.concatenate([low_ref[...], high_ref[...]], axis=0)
    for step, down in enumerate((own_ref[...], right_ref[...], far, left_ref[...])):
        owner = lax.rem(place_ref[0] + step, RING)
        z = dot(tok[:, :width], down, ((1,), (1,)))
        a = saved_ref[owner, way, 0].astype(F32)
        b = saved_ref[owner, way, 1].astype(F32)
        sig = jax.nn.sigmoid(a)
        act = a * sig
        total = total + act * b * z
        u = prob * z
        grad_gate = u * b * sig * (1.0 + a * (1.0 - sig))
        grads_ref[:, 2 * step * units : (2 * step + 1) * units] = grad_gate.astype(BF)
        grads_ref[:, (2 * step + 1) * units : (2 * step + 2) * units] = (u * act).astype(BF)
    scaled_ref[...] = jnp.sum(total, axis=1, keepdims=True) * (prob * (1.0 - prob))


def hidden_grads(way, place, tok, saved, down):
    planes, capacity, _ = tok.shape
    count, units = planes * capacity, saved.shape[4]
    whole = pl.BlockSpec(memory_space=pltpu.VMEM)
    return pl.pallas_call(
        functools.partial(hidden_kernel, way),
        in_specs=[pl.BlockSpec(memory_space=pltpu.SMEM)] + [whole] * (2 + len(down)),
        out_shape=[
            jax.ShapeDtypeStruct((count, 2 * RING * units), BF),
            jax.ShapeDtypeStruct((count, LANE), F32),
        ],
        compiler_params=pltpu.CompilerParams(vmem_limit_bytes=VMEM_LIMIT),
        cost_estimate=pl.CostEstimate(
            flops=10000000000, bytes_accessed=5 * 10**6, transcendentals=10**5
        ),
    )(place, tok, saved, *down)


def part_kernel(
    first_ref,
    first_scaled_ref,
    second_ref,
    second_scaled_ref,
    router_ref,
    own_ref,
    left_ref,
    right_ref,
    gate_ref,
    up_ref,
    out_ref,
):
    planes, two, width = out_ref.shape
    capacity = two // 2
    count = planes * capacity
    units = own_ref.shape[2]
    grads = jnp.concatenate([first_ref[...], second_ref[...]], axis=0)
    scaled = jnp.concatenate([first_scaled_ref[...], second_scaled_ref[...]], axis=0)[:, :1]
    block = width // 2
    for part in range(2):
        span = slice(part * block, (part + 1) * block)
        weights = (
            own_ref[0, span],
            own_ref[1, span],
            right_ref[0, span],
            right_ref[1, span],
            gate_ref[span],
            up_ref[span],
            left_ref[0, span],
            left_ref[1, span],
        )
        weights = jnp.concatenate(weights, axis=1)
        total = dot(grads, weights, ((1,), (1,))) + scaled * router_ref[:, span]
        total = total.astype(BF)
        for way in range(2):
            piece = total[way * count : (way + 1) * count].reshape(planes, capacity, block)
            out_ref[:, way * capacity : (way + 1) * capacity, span] = piece


def input_parts(flops, grads, router, weights, capacity):
    (first, first_scaled), (second, second_scaled) = grads
    width = router.shape[1]
    whole = pl.BlockSpec(memory_space=pltpu.VMEM)
    return pl.pallas_call(
        part_kernel,
        in_specs=[whole] * (5 + len(weights)),
        out_shape=jax.ShapeDtypeStruct((first.shape[0] // capacity, 2 * capacity, width), BF),
        compiler_params=pltpu.CompilerParams(vmem_limit_bytes=VMEM_LIMIT),
        cost_estimate=pl.CostEstimate(flops=flops, bytes_accessed=5 * 10**6, transcendentals=0),
    )(first, first_scaled, second, second_scaled, router, *weights)


def finish_kernel(experts, capacity, routes_ref, first_ref, second_ref, back_ref, *rest):
    out_ref = rest[-1]
    planes, _, width = back_ref.shape
    for way, grad_ref in enumerate((first_ref, second_ref)):
        select = selection(routes_ref[way, 0], planes // experts, capacity, experts).astype(BF)
        back = back_ref[:, way * capacity : (way + 1) * capacity].reshape(planes * capacity, width)
        back = dot(select, back, ((1,), (0,)))
        out_ref[way] = (grad_ref[...].astype(F32) + back).astype(BF)


def finish(part, routes, grads, back, experts, capacity, before):
    tokens, width = grads[0].shape
    block = back.shape[2]
    operands = [routes, *grads, back]
    specs = [
        pl.BlockSpec(routes.shape, lambda i: (0, 0, 0, 0)),
        pl.BlockSpec((tokens, block), lambda i: (0, part)),
        pl.BlockSpec((tokens, block), lambda i: (0, part)),
        pl.BlockSpec(back.shape, lambda i: (0, 0, 0)),
    ]
    aliases = {}
    if before is not None:
        operands.append(before)
        specs.append(pl.BlockSpec(memory_space=pl.ANY))
        aliases = {4: 0}
    return pl.pallas_call(
        functools.partial(finish_kernel, experts, capacity),
        grid=(1,),
        in_specs=specs,
        out_specs=pl.BlockSpec((2, tokens, block), lambda i: (0, 0, part)),
        out_shape=jax.ShapeDtypeStruct((2, tokens, width), BF),
        input_output_aliases=aliases,
        compiler_params=pltpu.CompilerParams(vmem_limit_bytes=VMEM_LIMIT),
        cost_estimate=pl.CostEstimate(flops=10**8, bytes_accessed=3 * 10**6, transcendentals=0),
    )(*operands)


def per_device(pending, routes, probs, saved_gate, saved_up, w_gate, w_up, w_down, w_router):
    members = lax.axis_size("expert")
    experts = w_router.shape[2]
    capacity = pending.shape[2] // experts
    me = lax.axis_index("expert")
    place = lax.rem(me, RING).reshape(1).astype(jnp.int32)
    expert = me // (members // experts)
    along_z, along_x = columns(members), rows(members)

    def exchange(value, groups):
        return lax.all_to_all(
            value, "expert", split_axis=0, concat_axis=0, axis_index_groups=groups, tiled=True
        )

    incoming = (shifted(pending[0, 0], "section", -1), shifted(pending[1, 0], "section", 1))
    saved = exchange(saved_blocks(saved_gate[:, 0, 0], saved_up[:, 0, 0]), along_x)

    width = w_gate.shape[1] // 2
    spans = [slice(part * width, (part + 1) * width) for part in range(2)]
    half = w_down.shape[1] // 2
    sent = list(pick(incoming, routes, probs, experts, capacity))
    own = w_down[0]
    wl, wr = turned(own, 1), turned(own, RING - 1)
    wf, wg = turned(wl[:half], 1), turned(wr[half:], RING - 1)
    down = (own, wl, wr, wf, wg)
    own = jnp.stack([w_gate[0, spans[0]], w_up[0, spans[0]]])

    al, ar = turned(own, 1), turned(own, RING - 1)
    af, ag = turned(al[0], 1), turned(ar[1], RING - 1)
    weights = [(own, al, ar, af, ag)]
    own = jnp.stack([w_gate[0, spans[1]], w_up[0, spans[1]]])
    own, _, _, _, _ = lax.optimization_barrier((own, al, ar, wf, wg))
    bl, br = turned(own, 1), turned(own, RING - 1)
    bf, bg = turned(bl[0], 1), turned(br[1], RING - 1)
    weights.append((own, bl, br, bf, bg))
    router = lax.dynamic_slice(w_router[0], (0, expert), (2 * width, 1)).reshape(1, 2 * width)

    sent[0], saved = lax.optimization_barrier((sent[0], saved))

    sent[1], _, _ = lax.optimization_barrier((sent[1], wl, wr))
    toks = [exchange(sent[way], along_z) for way in range(2)]


    grads = [hidden_grads(way, place, toks[way], saved, down) for way in range(2)]
    out = None
    for part in range(2):
        parts = input_parts(FLOPS[part], grads, router[:, spans[part]], weights[part], capacity)
        back = exchange(parts, along_z)
        out = finish(part, routes, incoming, back, experts, capacity, out)
    return out[:, None]


def solution(mesh):
    in_specs = (
        P(None, "section", "expert", None),
        P(None, "section", "expert", None),
        P(None, "section", "expert"),
        P(None, "section", "expert", None, None, None),
        P(None, "section", "expert", None, None, None),
        P("section", None, "expert"),
        P("section", None, "expert"),
        P("section", "expert", None),
        P("section", None, None),
    )
    out_specs = P(None, "section", "expert", None)
    return jax.shard_map(
        per_device, mesh=mesh, in_specs=in_specs, out_specs=out_specs, check_vma=False
    )
```

```python
import functools

import jax
import jax.numpy as jnp
from jax import lax
from jax.experimental import pallas as pl
from jax.experimental.pallas import tpu as pltpu
from jax.sharding import PartitionSpec as P

BF = jnp.bfloat16
F32 = jnp.float32
LANE = 128
FLOPS = (10000000000, 1000000000)
NEAR = 10**9
RING = 4
VMEM_LIMIT = 48 * 1024 * 1024


def shifted(value, axis, steps):
    count = lax.axis_size(axis)
    pairs = [(source, (source + steps) % count) for source in range(count)]
    return lax.ppermute(value, axis, pairs)


def turned(value, steps):
    count = lax.axis_size("expert")
    pairs = [(i, i - i % RING + (i + steps) % RING) for i in range(count)]
    return lax.ppermute(value, "expert", pairs)


def columns(count):
    return [[z * RING + x for z in range(count // RING)] for x in range(RING)]


def rows(count):
    return [[z * RING + x for x in range(RING)] for z in range(count // RING)]


def dot(a, b, contract):
    return lax.dot_general(a, b, ((contract[0], contract[1]), ((), ())), preferred_element_type=F32)


def selection(routes, copies, capacity, experts):
    count = routes.shape[0]
    width = experts * copies * capacity
    code = lax.broadcasted_iota(jnp.int32, (count, width), 1)
    chosen = routes == code // (copies * capacity)
    row = lax.broadcasted_iota(jnp.int32, (count, count), 0)
    col = lax.broadcasted_iota(jnp.int32, (count, count), 1)
    earlier = jnp.where(col < row, 1.0, 0.0).astype(BF)
    before = dot(earlier, jnp.where(chosen, 1.0, 0.0).astype(BF), ((1,), (0,)))
    return jnp.where(chosen & (before.astype(jnp.int32) == code % capacity), 1.0, 0.0)


def pick_kernel(experts, capacity, routes_ref, probs_ref, *rest):
    grads, outs = rest[:2], rest[2:]
    for way in range(2):
        tokens, width = grads[way].shape
        select = selection(routes_ref[way, 0], 1, capacity, experts)
        prob_row = jnp.broadcast_to(probs_ref[way].astype(F32), (tokens, tokens))
        row = lax.broadcasted_iota(jnp.int32, (tokens, tokens), 0)
        col = lax.broadcasted_iota(jnp.int32, (tokens, tokens), 1)
        prob_diag = jnp.where(row == col, prob_row, 0.0).astype(BF)
        select = select.astype(BF)
        prob = jnp.sum(dot(select, prob_diag, ((0,), (0,))), axis=1, keepdims=True)
        prob = jnp.broadcast_to(prob, (tokens, LANE)).astype(BF)
        step = width // RING
        for part in range(RING):
            span = slice(part * step, (part + 1) * step)
            picked = dot(select, grads[way][:, span], ((0,), (0,))).astype(BF)
            for place in range(2 * experts):
                first = place // 2 * capacity
                outs[way][place, :, span] = picked[first : first + capacity]
        for place in range(2 * experts):
            first = place // 2 * capacity
            outs[way][place, :, width:] = prob[first : first + capacity]


def pick(grads, routes, probs, experts, capacity):
    tokens, width = grads[0].shape
    return pl.pallas_call(
        functools.partial(pick_kernel, experts, capacity),
        out_shape=[jax.ShapeDtypeStruct((2 * experts, capacity, width + LANE), BF)] * 2,
        compiler_params=pltpu.CompilerParams(vmem_limit_bytes=VMEM_LIMIT),
        cost_estimate=pl.CostEstimate(flops=10**8, bytes_accessed=4 * 10**6, transcendentals=0),
    )(routes, probs, *grads)


def saved_kernel(gate_ref, up_ref, out_ref):
    planes, ring, capacity, units = gate_ref.shape[1:]
    for x in range(ring):
        for way in range(2):
            out_ref[x, way, 0] = gate_ref[way, :, x].reshape(planes * capacity, units)
            out_ref[x, way, 1] = up_ref[way, :, x].reshape(planes * capacity, units)


def saved_blocks(gate, up):
    _, senders, capacity, units = gate.shape
    planes = senders // RING
    gate = gate.reshape(2, planes, RING, capacity, units)
    up = up.reshape(2, planes, RING, capacity, units)
    return pl.pallas_call(
        saved_kernel,
        out_shape=jax.ShapeDtypeStruct((RING, 2, 2, planes * capacity, units), BF),
        compiler_params=pltpu.CompilerParams(vmem_limit_bytes=VMEM_LIMIT),
        cost_estimate=pl.CostEstimate(flops=0, bytes_accessed=2 * 10**6, transcendentals=0),
    )(gate, up)


def hidden_kernel(
    way, place_ref, tok_ref, saved_ref, own_ref, left_ref, right_ref, low_ref, high_ref, *outs
):
    grads_ref, scaled_ref = outs
    planes, capacity, wide = tok_ref.shape
    width = wide - LANE
    count = planes * capacity
    units = saved_ref.shape[4]
    tok = tok_ref[...].reshape(count, wide)
    prob = tok[:, width:].astype(F32)
    total = jnp.zeros((count, units), F32)
    far = jnp.concatenate([low_ref[...], high_ref[...]], axis=0)
    for step, down in enumerate((own_ref[...], right_ref[...], far, left_ref[...])):
        owner = lax.rem(place_ref[0] + step, RING)
        z = dot(tok[:, :width], down, ((1,), (1,)))
        a = saved_ref[owner, way, 0].astype(F32)
        b = saved_ref[owner, way, 1].astype(F32)
        sig = jax.nn.sigmoid(a)
        act = a * sig
        total = total + act * b * z
        u = prob * z
        grad_gate = u * b * sig * (1.0 + a * (1.0 - sig))
        grads_ref[:, 2 * step * units : (2 * step + 1) * units] = grad_gate.astype(BF)
        grads_ref[:, (2 * step + 1) * units : (2 * step + 2) * units] = (u * act).astype(BF)
    scaled_ref[...] = jnp.sum(total, axis=1, keepdims=True) * (prob * (1.0 - prob))


def hidden_grads(way, place, tok, saved, down):
    planes, capacity, _ = tok.shape
    count, units = planes * capacity, saved.shape[4]
    whole = pl.BlockSpec(memory_space=pltpu.VMEM)
    return pl.pallas_call(
        functools.partial(hidden_kernel, way),
        in_specs=[pl.BlockSpec(memory_space=pltpu.SMEM)] + [whole] * (2 + len(down)),
        out_shape=[
            jax.ShapeDtypeStruct((count, 2 * RING * units), BF),
            jax.ShapeDtypeStruct((count, LANE), F32),
        ],
        compiler_params=pltpu.CompilerParams(vmem_limit_bytes=VMEM_LIMIT),
        cost_estimate=pl.CostEstimate(
            flops=10000000000, bytes_accessed=5 * 10**6, transcendentals=10**5
        ),
    )(place, tok, saved, *down)


def part_kernel(
    first_ref,
    first_scaled_ref,
    second_ref,
    second_scaled_ref,
    router_ref,
    own_ref,
    left_ref,
    right_ref,
    gate_ref,
    up_ref,
    out_ref,
):
    planes, two, width = out_ref.shape
    capacity = two // 2
    count = planes * capacity
    units = own_ref.shape[2]
    grads = jnp.concatenate([first_ref[...], second_ref[...]], axis=0)
    scaled = jnp.concatenate([first_scaled_ref[...], second_scaled_ref[...]], axis=0)[:, :1]
    block = width // 2
    for part in range(2):
        span = slice(part * block, (part + 1) * block)
        weights = (
            own_ref[0, span],
            own_ref[1, span],
            right_ref[0, span],
            right_ref[1, span],
            gate_ref[span],
            up_ref[span],
            left_ref[0, span],
            left_ref[1, span],
        )
        weights = jnp.concatenate(weights, axis=1)
        total = dot(grads, weights, ((1,), (1,))) + scaled * router_ref[:, span]
        total = total.astype(BF)
        for way in range(2):
            piece = total[way * count : (way + 1) * count].reshape(planes, capacity, block)
            out_ref[:, way * capacity : (way + 1) * capacity, span] = piece


def input_parts(flops, grads, router, weights, capacity):
    (first, first_scaled), (second, second_scaled) = grads
    width = router.shape[1]
    whole = pl.BlockSpec(memory_space=pltpu.VMEM)
    return pl.pallas_call(
        part_kernel,
        in_specs=[whole] * (5 + len(weights)),
        out_shape=jax.ShapeDtypeStruct((first.shape[0] // capacity, 2 * capacity, width), BF),
        compiler_params=pltpu.CompilerParams(vmem_limit_bytes=VMEM_LIMIT),
        cost_estimate=pl.CostEstimate(flops=flops, bytes_accessed=5 * 10**6, transcendentals=0),
    )(first, first_scaled, second, second_scaled, router, *weights)


def near_kernel(
    first_ref,
    first_scaled_ref,
    second_ref,
    second_scaled_ref,
    router_ref,
    own_ref,
    left_ref,
    right_ref,
    out_ref,
):
    units = own_ref.shape[2]
    depth = 2 * units
    grads = jnp.concatenate([first_ref[...], second_ref[...]], axis=0)
    grads = jnp.concatenate([grads[:, : 2 * depth], grads[:, 3 * depth :]], axis=1)
    scaled = jnp.concatenate([first_scaled_ref[...], second_scaled_ref[...]], axis=0)[:, :1]
    block = out_ref.shape[1] // 2
    for part in range(2):
        span = slice(part * block, (part + 1) * block)
        weights = [ref[which, span] for ref in (own_ref, right_ref, left_ref) for which in range(2)]
        weights = jnp.concatenate(weights, axis=1)
        out_ref[:, span] = dot(grads, weights, ((1,), (1,))) + scaled * router_ref[:, span]


def far_kernel(first_ref, second_ref, near_ref, gate_ref, up_ref, out_ref):
    planes, two, width = out_ref.shape
    capacity = two // 2
    count = planes * capacity
    depth = 2 * gate_ref.shape[1]
    columns = slice(2 * depth, 3 * depth)
    grads = jnp.concatenate([first_ref[:, columns], second_ref[:, columns]], axis=0)
    block = width // 2
    for part in range(2):
        span = slice(part * block, (part + 1) * block)
        weights = jnp.concatenate([gate_ref[span], up_ref[span]], axis=1)
        total = (near_ref[:, span] + dot(grads, weights, ((1,), (1,)))).astype(BF)
        for way in range(2):
            piece = total[way * count : (way + 1) * count].reshape(planes, capacity, block)
            out_ref[:, way * capacity : (way + 1) * capacity, span] = piece


def late_parts(flops, grads, router, weights, capacity):
    (first, first_scaled), (second, second_scaled) = grads
    own, left, right, gate, up = weights
    width = router.shape[1]
    count = first.shape[0]
    whole = pl.BlockSpec(memory_space=pltpu.VMEM)
    params = pltpu.CompilerParams(vmem_limit_bytes=VMEM_LIMIT)
    near = pl.pallas_call(
        near_kernel,
        in_specs=[whole] * 8,
        out_specs=whole,
        out_shape=jax.ShapeDtypeStruct((2 * count, width), F32),
        compiler_params=params,
        cost_estimate=pl.CostEstimate(flops=NEAR, bytes_accessed=5 * 10**6, transcendentals=0),
    )(first, first_scaled, second, second_scaled, router, own, left, right)
    return pl.pallas_call(
        far_kernel,
        in_specs=[whole] * 5,
        out_shape=jax.ShapeDtypeStruct((count // capacity, 2 * capacity, width), BF),
        compiler_params=params,
        cost_estimate=pl.CostEstimate(flops=flops, bytes_accessed=5 * 10**6, transcendentals=0),
    )(first, second, near, gate, up)


def finish_kernel(experts, capacity, routes_ref, first_ref, second_ref, back_ref, *rest):
    out_ref = rest[-1]
    planes, _, width = back_ref.shape
    for way, grad_ref in enumerate((first_ref, second_ref)):
        select = selection(routes_ref[way, 0], planes // experts, capacity, experts).astype(BF)
        back = back_ref[:, way * capacity : (way + 1) * capacity].reshape(planes * capacity, width)
        back = dot(select, back, ((1,), (0,)))
        out_ref[way] = (grad_ref[...].astype(F32) + back).astype(BF)


def finish(part, routes, grads, back, experts, capacity, before):
    tokens, width = grads[0].shape
    block = back.shape[2]
    operands = [routes, *grads, back]
    specs = [
        pl.BlockSpec(routes.shape, lambda i: (0, 0, 0, 0)),
        pl.BlockSpec((tokens, block), lambda i: (0, part)),
        pl.BlockSpec((tokens, block), lambda i: (0, part)),
        pl.BlockSpec(back.shape, lambda i: (0, 0, 0)),
    ]
    aliases = {}
    if before is not None:
        operands.append(before)
        specs.append(pl.BlockSpec(memory_space=pl.ANY))
        aliases = {4: 0}
    return pl.pallas_call(
        functools.partial(finish_kernel, experts, capacity),
        grid=(1,),
        in_specs=specs,
        out_specs=pl.BlockSpec((2, tokens, block), lambda i: (0, 0, part)),
        out_shape=jax.ShapeDtypeStruct((2, tokens, width), BF),
        input_output_aliases=aliases,
        compiler_params=pltpu.CompilerParams(vmem_limit_bytes=VMEM_LIMIT),
        cost_estimate=pl.CostEstimate(flops=10**8, bytes_accessed=3 * 10**6, transcendentals=0),
    )(*operands)


def per_device(pending, routes, probs, saved_gate, saved_up, w_gate, w_up, w_down, w_router):
    members = lax.axis_size("expert")
    experts = w_router.shape[2]
    capacity = pending.shape[2] // experts
    me = lax.axis_index("expert")
    place = lax.rem(me, RING).reshape(1).astype(jnp.int32)
    expert = me // (members // experts)
    along_z, along_x = columns(members), rows(members)

    def exchange(value, groups):
        return lax.all_to_all(
            value, "expert", split_axis=0, concat_axis=0, axis_index_groups=groups, tiled=True
        )

    incoming = (shifted(pending[0, 0], "section", -1), shifted(pending[1, 0], "section", 1))
    saved = exchange(saved_blocks(saved_gate[:, 0, 0], saved_up[:, 0, 0]), along_x)

    width = w_gate.shape[1] // 2
    spans = [slice(part * width, (part + 1) * width) for part in range(2)]
    half = w_down.shape[1] // 2
    sent = list(pick(incoming, routes, probs, experts, capacity))
    own = w_down[0]
    wl, wr = turned(own, 1), turned(own, RING - 1)
    wf, wg = turned(wl[:half], 1), turned(wr[half:], RING - 1)
    down = (own, wl, wr, wf, wg)
    own = jnp.stack([w_gate[0, spans[0]], w_up[0, spans[0]]])

    al, ar = turned(own, 1), turned(own, RING - 1)
    af, ag = turned(al[0], 1), turned(ar[1], RING - 1)
    weights = [(own, al, ar, af, ag)]
    own = jnp.stack([w_gate[0, spans[1]], w_up[0, spans[1]]])
    own, _, _, _, _ = lax.optimization_barrier((own, al, ar, wf, wg))
    bl, br = turned(own, 1), turned(own, RING - 1)
    bf, bg = turned(bl[0], 1), turned(br[1], RING - 1)
    weights.append((own, bl, br, bf, bg))
    router = lax.dynamic_slice(w_router[0], (0, expert), (2 * width, 1)).reshape(1, 2 * width)

    sent[0], saved = lax.optimization_barrier((sent[0], saved))

    sent[1], _, _ = lax.optimization_barrier((sent[1], wl, wr))
    toks = [exchange(sent[way], along_z) for way in range(2)]


    grads = [hidden_grads(way, place, toks[way], saved, down) for way in range(2)]
    out = None
    for part in range(2):
        compute = input_parts if part == 0 else late_parts
        parts = compute(FLOPS[part], grads, router[:, spans[part]], weights[part], capacity)
        back = exchange(parts, along_z)
        out = finish(part, routes, incoming, back, experts, capacity, out)
    return out[:, None]


def solution(mesh):
    in_specs = (
        P(None, "section", "expert", None),
        P(None, "section", "expert", None),
        P(None, "section", "expert"),
        P(None, "section", "expert", None, None, None),
        P(None, "section", "expert", None, None, None),
        P("section", None, "expert"),
        P("section", None, "expert"),
        P("section", "expert", None),
        P("section", None, None),
    )
    out_specs = P(None, "section", "expert", None)
    return jax.shard_map(
        per_device, mesh=mesh, in_specs=in_specs, out_specs=out_specs, check_vma=False
    )
```

```python
import functools

import jax
import jax.numpy as jnp
from jax import lax
from jax.experimental import pallas as pl
from jax.experimental.pallas import tpu as pltpu
from jax.sharding import PartitionSpec as P

BF = jnp.bfloat16
F32 = jnp.float32
LANE = 128
FLOPS = (10000000000, 1000000000)
NEAR = 10**9
RING = 4
VMEM_LIMIT = 24 * 1024 * 1024


def shifted(value, axis, steps):
    count = lax.axis_size(axis)
    pairs = [(source, (source + steps) % count) for source in range(count)]
    return lax.ppermute(value, axis, pairs)


def turned(value, steps):
    count = lax.axis_size("expert")
    pairs = [(i, i - i % RING + (i + steps) % RING) for i in range(count)]
    return lax.ppermute(value, "expert", pairs)


def columns(count):
    return [[z * RING + x for z in range(count // RING)] for x in range(RING)]


def rows(count):
    return [[z * RING + x for x in range(RING)] for z in range(count // RING)]


def dot(a, b, contract):
    return lax.dot_general(a, b, ((contract[0], contract[1]), ((), ())), preferred_element_type=F32)


def selection(routes, copies, capacity, experts):
    count = routes.shape[0]
    width = experts * copies * capacity
    code = lax.broadcasted_iota(jnp.int32, (count, width), 1)
    chosen = routes == code // (copies * capacity)
    row = lax.broadcasted_iota(jnp.int32, (count, count), 0)
    col = lax.broadcasted_iota(jnp.int32, (count, count), 1)
    earlier = jnp.where(col < row, 1.0, 0.0).astype(BF)
    before = dot(earlier, jnp.where(chosen, 1.0, 0.0).astype(BF), ((1,), (0,)))
    return jnp.where(chosen & (before.astype(jnp.int32) == code % capacity), 1.0, 0.0)


def pick_kernel(experts, capacity, routes_ref, probs_ref, *rest):
    grads, outs = rest[:2], rest[2:]
    for way in range(2):
        tokens, width = grads[way].shape
        select = selection(routes_ref[way, 0], 1, capacity, experts)
        prob_row = jnp.broadcast_to(probs_ref[way].astype(F32), (tokens, tokens))
        row = lax.broadcasted_iota(jnp.int32, (tokens, tokens), 0)
        col = lax.broadcasted_iota(jnp.int32, (tokens, tokens), 1)
        prob_diag = jnp.where(row == col, prob_row, 0.0).astype(BF)
        select = select.astype(BF)
        prob = jnp.sum(dot(select, prob_diag, ((0,), (0,))), axis=1, keepdims=True)
        prob = jnp.broadcast_to(prob, (tokens, LANE)).astype(BF)
        step = width // RING
        for part in range(RING):
            span = slice(part * step, (part + 1) * step)
            picked = dot(select, grads[way][:, span], ((0,), (0,))).astype(BF)
            for place in range(2 * experts):
                first = place // 2 * capacity
                outs[way][place, :, span] = picked[first : first + capacity]
        for place in range(2 * experts):
            first = place // 2 * capacity
            outs[way][place, :, width:] = prob[first : first + capacity]


def pick(grads, routes, probs, experts, capacity):
    tokens, width = grads[0].shape
    return pl.pallas_call(
        functools.partial(pick_kernel, experts, capacity),
        out_shape=[jax.ShapeDtypeStruct((2 * experts, capacity, width + LANE), BF)] * 2,
        compiler_params=pltpu.CompilerParams(vmem_limit_bytes=VMEM_LIMIT),
        cost_estimate=pl.CostEstimate(flops=10**8, bytes_accessed=4 * 10**6, transcendentals=0),
    )(routes, probs, *grads)


def saved_kernel(gate_ref, up_ref, out_ref):
    planes, ring, capacity, units = gate_ref.shape[1:]
    for x in range(ring):
        for way in range(2):
            out_ref[x, way, 0] = gate_ref[way, :, x].reshape(planes * capacity, units)
            out_ref[x, way, 1] = up_ref[way, :, x].reshape(planes * capacity, units)


def saved_blocks(gate, up):
    _, senders, capacity, units = gate.shape
    planes = senders // RING
    gate = gate.reshape(2, planes, RING, capacity, units)
    up = up.reshape(2, planes, RING, capacity, units)
    return pl.pallas_call(
        saved_kernel,
        out_shape=jax.ShapeDtypeStruct((RING, 2, 2, planes * capacity, units), BF),
        compiler_params=pltpu.CompilerParams(vmem_limit_bytes=VMEM_LIMIT),
        cost_estimate=pl.CostEstimate(flops=0, bytes_accessed=2 * 10**6, transcendentals=0),
    )(gate, up)


def hidden_kernel(
    way, place_ref, tok_ref, saved_ref, own_ref, left_ref, right_ref, low_ref, high_ref, *outs
):
    grads_ref, scaled_ref = outs
    planes, capacity, wide = tok_ref.shape
    width = wide - LANE
    count = planes * capacity
    units = saved_ref.shape[4]
    tok = tok_ref[...].reshape(count, wide)
    prob = tok[:, width:].astype(F32)
    total = jnp.zeros((count, units), F32)
    far = jnp.concatenate([low_ref[...], high_ref[...]], axis=0)
    for step, down in enumerate((own_ref[...], right_ref[...], far, left_ref[...])):
        owner = lax.rem(place_ref[0] + step, RING)
        z = dot(tok[:, :width], down, ((1,), (1,)))
        a = saved_ref[owner, way, 0].astype(F32)
        b = saved_ref[owner, way, 1].astype(F32)
        sig = jax.nn.sigmoid(a)
        act = a * sig
        total = total + act * b * z
        u = prob * z
        grad_gate = u * b * sig * (1.0 + a * (1.0 - sig))
        grads_ref[:, 2 * step * units : (2 * step + 1) * units] = grad_gate.astype(BF)
        grads_ref[:, (2 * step + 1) * units : (2 * step + 2) * units] = (u * act).astype(BF)
    scaled_ref[...] = jnp.sum(total, axis=1, keepdims=True) * (prob * (1.0 - prob))


def hidden_grads(way, place, tok, saved, down):
    planes, capacity, _ = tok.shape
    count, units = planes * capacity, saved.shape[4]
    whole = pl.BlockSpec(memory_space=pltpu.VMEM)
    return pl.pallas_call(
        functools.partial(hidden_kernel, way),
        in_specs=[pl.BlockSpec(memory_space=pltpu.SMEM)] + [whole] * (2 + len(down)),
        out_shape=[
            jax.ShapeDtypeStruct((count, 2 * RING * units), BF),
            jax.ShapeDtypeStruct((count, LANE), F32),
        ],
        compiler_params=pltpu.CompilerParams(vmem_limit_bytes=VMEM_LIMIT),
        cost_estimate=pl.CostEstimate(
            flops=10000000000, bytes_accessed=5 * 10**6, transcendentals=10**5
        ),
    )(place, tok, saved, *down)


def part_kernel(
    first_ref,
    first_scaled_ref,
    second_ref,
    second_scaled_ref,
    router_ref,
    own_ref,
    left_ref,
    right_ref,
    gate_ref,
    up_ref,
    out_ref,
):
    planes, two, width = out_ref.shape
    capacity = two // 2
    count = planes * capacity
    units = own_ref.shape[2]
    grads = jnp.concatenate([first_ref[...], second_ref[...]], axis=0)
    scaled = jnp.concatenate([first_scaled_ref[...], second_scaled_ref[...]], axis=0)[:, :1]
    block = width // 2
    for part in range(2):
        span = slice(part * block, (part + 1) * block)
        weights = (
            own_ref[0, span],
            own_ref[1, span],
            right_ref[0, span],
            right_ref[1, span],
            gate_ref[span],
            up_ref[span],
            left_ref[0, span],
            left_ref[1, span],
        )
        weights = jnp.concatenate(weights, axis=1)
        total = dot(grads, weights, ((1,), (1,))) + scaled * router_ref[:, span]
        total = total.astype(BF)
        for way in range(2):
            piece = total[way * count : (way + 1) * count].reshape(planes, capacity, block)
            out_ref[:, way * capacity : (way + 1) * capacity, span] = piece


def input_parts(flops, grads, router, weights, capacity):
    (first, first_scaled), (second, second_scaled) = grads
    width = router.shape[1]
    whole = pl.BlockSpec(memory_space=pltpu.VMEM)
    return pl.pallas_call(
        part_kernel,
        in_specs=[whole] * (5 + len(weights)),
        out_shape=jax.ShapeDtypeStruct((first.shape[0] // capacity, 2 * capacity, width), BF),
        compiler_params=pltpu.CompilerParams(vmem_limit_bytes=VMEM_LIMIT),
        cost_estimate=pl.CostEstimate(flops=flops, bytes_accessed=5 * 10**6, transcendentals=0),
    )(first, first_scaled, second, second_scaled, router, *weights)


def near_kernel(
    first_ref,
    first_scaled_ref,
    second_ref,
    second_scaled_ref,
    router_ref,
    own_ref,
    left_ref,
    right_ref,
    out_ref,
):
    units = own_ref.shape[2]
    depth = 2 * units
    grads = jnp.concatenate([first_ref[...], second_ref[...]], axis=0)
    grads = jnp.concatenate([grads[:, : 2 * depth], grads[:, 3 * depth :]], axis=1)
    scaled = jnp.concatenate([first_scaled_ref[...], second_scaled_ref[...]], axis=0)[:, :1]
    block = out_ref.shape[1] // 2
    for part in range(2):
        span = slice(part * block, (part + 1) * block)
        weights = [ref[which, span] for ref in (own_ref, right_ref, left_ref) for which in range(2)]
        weights = jnp.concatenate(weights, axis=1)
        out_ref[:, span] = dot(grads, weights, ((1,), (1,))) + scaled * router_ref[:, span]


def far_kernel(first_ref, second_ref, near_ref, gate_ref, up_ref, out_ref):
    planes, two, width = out_ref.shape
    capacity = two // 2
    count = planes * capacity
    depth = 2 * gate_ref.shape[1]
    columns = slice(2 * depth, 3 * depth)
    grads = jnp.concatenate([first_ref[:, columns], second_ref[:, columns]], axis=0)
    block = width // 2
    for part in range(2):
        span = slice(part * block, (part + 1) * block)
        weights = jnp.concatenate([gate_ref[span], up_ref[span]], axis=1)
        total = (near_ref[:, span] + dot(grads, weights, ((1,), (1,)))).astype(BF)
        for way in range(2):
            piece = total[way * count : (way + 1) * count].reshape(planes, capacity, block)
            out_ref[:, way * capacity : (way + 1) * capacity, span] = piece


def late_parts(flops, grads, router, weights, capacity):
    (first, first_scaled), (second, second_scaled) = grads
    own, left, right, gate, up = weights
    width = router.shape[1]
    count = first.shape[0]
    whole = pl.BlockSpec(memory_space=pltpu.VMEM)
    params = pltpu.CompilerParams(vmem_limit_bytes=VMEM_LIMIT)
    near = pl.pallas_call(
        near_kernel,
        in_specs=[whole] * 8,
        out_specs=whole,
        out_shape=jax.ShapeDtypeStruct((2 * count, width), F32),
        compiler_params=params,
        cost_estimate=pl.CostEstimate(flops=NEAR, bytes_accessed=5 * 10**6, transcendentals=0),
    )(first, first_scaled, second, second_scaled, router, own, left, right)
    return pl.pallas_call(
        far_kernel,
        in_specs=[whole] * 5,
        out_shape=jax.ShapeDtypeStruct((count // capacity, 2 * capacity, width), BF),
        compiler_params=params,
        cost_estimate=pl.CostEstimate(flops=flops, bytes_accessed=5 * 10**6, transcendentals=0),
    )(first, second, near, gate, up)


def finish_kernel(experts, capacity, routes_ref, first_ref, second_ref, back_ref, *rest):
    out_ref = rest[-1]
    planes, _, width = back_ref.shape
    for way, grad_ref in enumerate((first_ref, second_ref)):
        select = selection(routes_ref[way, 0], planes // experts, capacity, experts).astype(BF)
        back = back_ref[:, way * capacity : (way + 1) * capacity].reshape(planes * capacity, width)
        back = dot(select, back, ((1,), (0,)))
        out_ref[way] = (grad_ref[...].astype(F32) + back).astype(BF)


def finish(part, routes, grads, back, experts, capacity, before):
    tokens, width = grads[0].shape
    block = back.shape[2]
    operands = [routes, *grads, back]
    specs = [
        pl.BlockSpec(routes.shape, lambda i: (0, 0, 0, 0)),
        pl.BlockSpec((tokens, block), lambda i: (0, part)),
        pl.BlockSpec((tokens, block), lambda i: (0, part)),
        pl.BlockSpec(back.shape, lambda i: (0, 0, 0)),
    ]
    aliases = {}
    if before is not None:
        operands.append(before)
        specs.append(pl.BlockSpec(memory_space=pl.ANY))
        aliases = {4: 0}
    return pl.pallas_call(
        functools.partial(finish_kernel, experts, capacity),
        grid=(1,),
        in_specs=specs,
        out_specs=pl.BlockSpec((2, tokens, block), lambda i: (0, 0, part)),
        out_shape=jax.ShapeDtypeStruct((2, tokens, width), BF),
        input_output_aliases=aliases,
        compiler_params=pltpu.CompilerParams(vmem_limit_bytes=VMEM_LIMIT),
        cost_estimate=pl.CostEstimate(flops=10**8, bytes_accessed=3 * 10**6, transcendentals=0),
    )(*operands)


def per_device(pending, routes, probs, saved_gate, saved_up, w_gate, w_up, w_down, w_router):
    members = lax.axis_size("expert")
    experts = w_router.shape[2]
    capacity = pending.shape[2] // experts
    me = lax.axis_index("expert")
    place = lax.rem(me, RING).reshape(1).astype(jnp.int32)
    expert = me // (members // experts)
    along_z, along_x = columns(members), rows(members)

    def exchange(value, groups):
        return lax.all_to_all(
            value, "expert", split_axis=0, concat_axis=0, axis_index_groups=groups, tiled=True
        )

    incoming = (shifted(pending[0, 0], "section", -1), shifted(pending[1, 0], "section", 1))
    saved = exchange(saved_blocks(saved_gate[:, 0, 0], saved_up[:, 0, 0]), along_x)

    width = w_gate.shape[1] // 2
    spans = [slice(part * width, (part + 1) * width) for part in range(2)]
    half = w_down.shape[1] // 2
    sent = list(pick(incoming, routes, probs, experts, capacity))
    own = w_down[0]
    wl, wr = turned(own, 1), turned(own, RING - 1)
    wf, wg = turned(wl[:half], 1), turned(wr[half:], RING - 1)
    down = (own, wl, wr, wf, wg)
    own = jnp.stack([w_gate[0, spans[0]], w_up[0, spans[0]]])

    al, ar = turned(own, 1), turned(own, RING - 1)
    af, ag = turned(al[0], 1), turned(ar[1], RING - 1)
    weights = [(own, al, ar, af, ag)]
    own = jnp.stack([w_gate[0, spans[1]], w_up[0, spans[1]]])
    own, _, _, _, _ = lax.optimization_barrier((own, al, ar, wf, wg))
    bl, br = turned(own, 1), turned(own, RING - 1)
    bf, bg = turned(bl[0], 1), turned(br[1], RING - 1)
    weights.append((own, bl, br, bf, bg))
    router = lax.dynamic_slice(w_router[0], (0, expert), (2 * width, 1)).reshape(1, 2 * width)

    sent[0], saved = lax.optimization_barrier((sent[0], saved))

    sent[1], _, _ = lax.optimization_barrier((sent[1], wl, wr))
    toks = [exchange(sent[way], along_z) for way in range(2)]


    grads = [hidden_grads(way, place, toks[way], saved, down) for way in range(2)]
    out = None
    for part in range(2):
        compute = input_parts if part == 0 else late_parts
        parts = compute(FLOPS[part], grads, router[:, spans[part]], weights[part], capacity)
        back = exchange(parts, along_z)
        out = finish(part, routes, incoming, back, experts, capacity, out)
    return out[:, None]


def solution(mesh):
    in_specs = (
        P(None, "section", "expert", None),
        P(None, "section", "expert", None),
        P(None, "section", "expert"),
        P(None, "section", "expert", None, None, None),
        P(None, "section", "expert", None, None, None),
        P("section", None, "expert"),
        P("section", None, "expert"),
        P("section", "expert", None),
        P("section", None, None),
    )
    out_specs = P(None, "section", "expert", None)
    return jax.shard_map(
        per_device, mesh=mesh, in_specs=in_specs, out_specs=out_specs, check_vma=False
    )
```
